256 devices in a mesh: blk: 256 (over x, y, z, core).
Axes of the slice: x: 4, y: 4, z: 8, core: 2. Of those that a mesh axis runs over, the one named last changes fastest.
Arguments:
- points: bfloat16 [262144, 128], P('blk'), may hold values from -6 to 6
- w_input: bfloat16 [128, 128], replicated, may hold values from -0.5 to 0.5
- w_output: bfloat16 [128, 128], replicated, may hold values from -0.5 to 0.5
- vectors: bfloat16 [17, 262144], P(None, 'blk'), may hold values from -0.5 to 0.5
- adjoint: bfloat16 [17, 262144], P(None, 'blk'), may hold values from -0.5 to 0.5
Outputs:
- products: float32 [17, 262144], P(None, 'blk')
- grad_input: float32 [128, 128], replicated
- grad_output: float32 [128, 128], replicated
The draws below stay inside these ranges and needn't reach their ends.
All inputs are finite; a program needn't handle non-finite values.
Results may differ from the reference program's by a relative error of at most 0.014.
Values may be sent and summed in bfloat16 or wider, within the bound.
No kernel may reach another device: no remote copies, remote signals or barrier semaphores. Data moves between devices by JAX's collectives and lax.ppermute only.
A program may use at most 64 MiB of HBM per device.

```python
import jax
import jax.numpy as jnp
from jax import lax

DIN = 128
HID = 128
FEAT = 128
NVEC = 17
ROUNDS = 4
BLOCK = 1024
N_POINTS = 262144
N_BLK = 256


def steps_of(own_key, dims, shards, smallest, high):
    level = 1.0
    for dim, shards_of in shards:
        draws = jax.random.uniform(jax.random.fold_in(jax.random.fold_in(own_key, 6), dim), (shards_of,), jnp.float32, smallest / len(shards), high / len(shards))
        level = level * jnp.repeat(jnp.exp(draws), dims[dim] // shards_of).reshape((-1,) + (1,) * (len(dims) - 1 - dim))
    return level


def scatter_about(key, dims, spread, limit, cuts=(), held_as=jnp.bfloat16):
    result = jax.random.normal(key, dims, jnp.float32) * spread
    if len(cuts) > 0:
        result = steps_of(key, dims, cuts, -0.22, 0.18) * result
    return jnp.clip(result, min=-limit, max=limit).astype(held_as)


def setup_inputs(seed: int = 0) -> dict:
    keys = jax.random.split(jax.random.key(seed), 6)
    return {
        "points": scatter_about(keys[0], (N_POINTS, DIN), 1.0, 6.0, ((0, 256),)),
        "w_input": scatter_about(keys[1], (DIN, HID), DIN ** -0.5, 0.5),
        "w_output": scatter_about(keys[2], (HID, FEAT), HID ** -0.5, 0.5),
        "vectors": scatter_about(keys[3], (NVEC, N_POINTS), (BLOCK ** -0.5), 0.5, ((1, 256),)),
        "adjoint": scatter_about(keys[4], (NVEC, N_POINTS), (16 * N_POINTS ** -0.5), 0.5, ((1, 256),)),
    }


def tile_terms(row_feats, row_adj, row_vec, col_feats, col_adj, col_vec):
    kernel_scale = row_feats.shape[1] / 4.0
    row_sq = jnp.sum(jnp.square(row_feats.astype(jnp.float32)), axis=1)
    col_sq = jnp.sum(jnp.square(col_feats.astype(jnp.float32)), axis=1)
    inner = jnp.dot(row_feats.astype(jnp.float32), col_feats.astype(jnp.float32).T)
    distance = row_sq[:, None] + col_sq[None, :] - 2.0 * inner
    kernel = jnp.exp(-distance / kernel_scale)
    kernel_b = kernel.astype(jnp.bfloat16)
    row_prod = jnp.dot(col_vec.astype(jnp.float32), kernel_b.astype(jnp.float32).T)
    left = jnp.concatenate([row_adj, row_vec], axis=0).astype(jnp.float32)
    right = jnp.concatenate([col_vec, col_adj], axis=0).astype(jnp.float32)
    pairing = jnp.dot(left.T, right)
    weight = pairing * kernel
    weight_b = weight.astype(jnp.bfloat16)
    row_grad = (-2.0 / kernel_scale) * (jnp.sum(weight, axis=1)[:, None] * row_feats.astype(jnp.float32)
                                        - jnp.dot(weight_b.astype(jnp.float32), col_feats.astype(jnp.float32)))
    return row_prod, row_grad


def reference(points, w_input, w_output, vectors, adjoint):
    preact = jnp.dot(points, w_input, preferred_element_type=jnp.float32)
    hidden = jnp.tanh(preact).astype(jnp.bfloat16)
    feats = jnp.dot(hidden, w_output, preferred_element_type=jnp.float32).astype(jnp.bfloat16)

    def block_data(block):
        start = (block * BLOCK).astype(jnp.int32)
        return (lax.dynamic_slice_in_dim(feats, start, BLOCK, 0),
                lax.dynamic_slice_in_dim(adjoint, start, BLOCK, 1),
                lax.dynamic_slice_in_dim(vectors, start, BLOCK, 1))

    def one_block(block):
        own_f, own_a, own_v = block_data(block)
        prod_sum, grad_sum = tile_terms(own_f, own_a, own_v, own_f, own_a, own_v)
        for level in range(ROUNDS):
            partner = jnp.bitwise_xor(block, jnp.int32(2 ** level)).astype(jnp.int32)
            other_f, other_a, other_v = block_data(partner)
            row_prod, row_grad = tile_terms(own_f, own_a, own_v, other_f, other_a, other_v)
            prod_sum = prod_sum + row_prod
            grad_sum = grad_sum + row_grad
        return prod_sum, grad_sum

    blocks = jnp.arange(N_BLK, dtype=jnp.int32)
    all_prods, all_grads = lax.map(one_block, blocks)
    products = jnp.transpose(all_prods, (1, 0, 2)).reshape(NVEC, N_POINTS)
    feat_grad_b = all_grads.reshape(N_POINTS, FEAT).astype(jnp.bfloat16)
    grad_output = jnp.dot(hidden.T, feat_grad_b, preferred_element_type=jnp.float32)
    back = jnp.dot(feat_grad_b, w_output.T, preferred_element_type=jnp.float32)
    hidden_f = hidden.astype(jnp.float32)
    hidden_grad = (back * (1.0 - hidden_f * hidden_f)).astype(jnp.bfloat16)
    grad_input = jnp.dot(points.T, hidden_grad, preferred_element_type=jnp.float32)
    return products, grad_input, grad_output
```

```python
import jax
import jax.numpy as jnp
from jax import lax
from jax.sharding import Mesh, PartitionSpec as P

ROUNDS = 4
ALL = ("x", "y", "z", "c")


def from_partner(x, distance):
    return lax.ppermute(x, ALL, [(i, i ^ 1 << distance) for i in range(lax.axis_size(ALL))])


def swap_cores(x):
    return lax.ppermute(x, "c", [(0, 1), (1, 0)])


def sum_over(x, axes):
    n = lax.axis_size(axes)
    sent = jnp.broadcast_to(x.astype(jnp.bfloat16), (n,) + x.shape)
    got = lax.all_to_all(sent, axes, 0, 0)
    return jnp.sum(got.astype(jnp.float32), axis=0)


def tile_terms(row_feats, row_adj, row_vec, col_feats, col_adj, col_vec):
    kernel_scale = row_feats.shape[1] / 4.0
    row_sq = jnp.sum(jnp.square(row_feats.astype(jnp.float32)), axis=1)
    col_sq = jnp.sum(jnp.square(col_feats.astype(jnp.float32)), axis=1)
    inner = lax.dot_general(
        row_feats, col_feats, (((1,), (1,)), ((), ())), preferred_element_type=jnp.float32
    )
    distance = row_sq[:, None] + col_sq[None, :] - 2.0 * inner
    kernel = jnp.exp(-distance / kernel_scale)
    kernel_b = kernel.astype(jnp.bfloat16)
    row_prod = lax.dot_general(
        col_vec, kernel_b, (((1,), (1,)), ((), ())), preferred_element_type=jnp.float32
    )
    left = jnp.concatenate([row_adj, row_vec], axis=0)
    right = jnp.concatenate([col_vec, col_adj], axis=0)
    pairing = lax.dot_general(
        left, right, (((0,), (0,)), ((), ())), preferred_element_type=jnp.float32
    )
    weight = pairing * kernel
    weight_b = weight.astype(jnp.bfloat16)
    factor = -2.0 / kernel_scale
    row_grad = factor * (
        jnp.sum(weight, axis=1)[:, None] * row_feats.astype(jnp.float32)
        - jnp.dot(weight_b, col_feats, preferred_element_type=jnp.float32)
    )
    return (row_prod, row_grad)


def local(points, w_input, w_output, vectors, adjoint):
    preact = jnp.dot(points, w_input, preferred_element_type=jnp.float32)
    hidden = jnp.tanh(preact).astype(jnp.bfloat16)
    feats = jnp.dot(hidden, w_output, preferred_element_type=jnp.float32).astype(jnp.bfloat16)
    prod_sum, grad_sum = tile_terms(feats, adjoint, vectors, feats, adjoint, vectors)
    for level in range(ROUNDS):
        other_feats, other_adj, other_vec = from_partner((feats, adjoint, vectors), level)
        row_prod, row_grad = tile_terms(feats, adjoint, vectors, other_feats, other_adj, other_vec)
        prod_sum = prod_sum + row_prod
        grad_sum = grad_sum + row_grad
    feat_grad_b = grad_sum.astype(jnp.bfloat16)
    local_output = lax.dot_general(
        hidden, feat_grad_b, (((0,), (0,)), ((), ())), preferred_element_type=jnp.float32
    )
    back = lax.dot_general(
        feat_grad_b, w_output, (((1,), (1,)), ((), ())), preferred_element_type=jnp.float32
    )
    hidden_f = hidden.astype(jnp.float32)
    hidden_grad = (back * (1.0 - hidden_f * hidden_f)).astype(jnp.bfloat16)
    local_input = lax.dot_general(
        points, hidden_grad, (((0,), (0,)), ((), ())), preferred_element_type=jnp.float32
    )
    second = lax.axis_index("c") == 1
    mine = jnp.where(second, local_output, local_input)
    mine = mine + swap_cores(jnp.where(second, local_input, local_output))
    mine = sum_over(mine, ("z",))
    mine = sum_over(mine, ("x", "y"))
    other = swap_cores(mine)
    grad_input = jnp.where(second, other, mine)
    grad_output = jnp.where(second, mine, other)
    return (prod_sum, grad_input, grad_output)


def solution(mesh):
    grid = Mesh(mesh.devices.reshape(4, 4, 8, 2), ALL)
    return jax.shard_map(
        local,
        mesh=grid,
        in_specs=(P(ALL, None), P(), P(), P(None, ALL), P(None, ALL)),
        out_specs=(P(None, ALL), P(), P()),
        check_vma=False,
    )
```

```python
import functools
import math

import jax
import jax.numpy as jnp
from jax import lax
from jax.experimental import pallas as pl
from jax.experimental.pallas import tpu as pltpu
from jax.sharding import Mesh, PartitionSpec as P

ALL = ("x", "y", "z", "c")
CHUNK = 256
LOG2E = math.log2(math.e)
F32 = jnp.float32
BF16 = jnp.bfloat16


def bit(i, k):
    return (i >> k) & 1


def far_target(i):
    return i ^ 8 if bit(i, 3) ^ bit(i, 2) ^ bit(i, 0) == 0 else i ^ 4


def near_target(i):
    return i ^ 1 if bit(i, 1) ^ bit(i, 0) == 0 else i ^ 2


def send(x, target):
    return lax.ppermute(x, ALL, [(i, target(i)) for i in range(lax.axis_size(ALL))])


def send_back(x, target):
    return lax.ppermute(x, ALL, [(target(i), i) for i in range(lax.axis_size(ALL))])


def swap_cores(x):
    return lax.ppermute(x, "c", [(0, 1), (1, 0)])


def sum_over(x, axes):
    n = lax.axis_size(axes)
    sent = jnp.broadcast_to(x.astype(BF16), (n,) + x.shape)
    got = lax.all_to_all(sent, axes, 0, 0)
    return jnp.sum(got.astype(F32), axis=0)


def dot(a, b):
    return jnp.dot(a, b, preferred_element_type=F32)


def dot_nt(a, b):
    return lax.dot_general(a, b, (((1,), (1,)), ((), ())), preferred_element_type=F32)


def forward(pts, w_in, w_out):
    hid_t = jnp.tanh(dot_nt(w_in.astype(F32).T.astype(BF16), pts)).astype(BF16)
    feats_t = dot(w_out.astype(F32).T.astype(BF16), hid_t).astype(BF16)
    n = pts.shape[0]
    ones = (lax.broadcasted_iota(jnp.int32, (16, n), 0) == 0).astype(F32).astype(BF16)
    return hid_t, feats_t, jnp.concatenate([feats_t, ones], axis=0)


def half_square(feats, axis, feat):
    return jnp.sum(jnp.square(feats.astype(F32)), axis=axis, keepdims=True) * (-LOG2E / (feat / 4.0))


def kernel_and_weight(rows, row_sq, row_av, col_feats_t, col_sq, col_va, feat):
    inner = dot(rows, col_feats_t)
    kernel = jnp.exp2(inner * (2.0 * LOG2E / (feat / 4.0)) + (row_sq + col_sq))
    weight = dot(row_av, col_va) * kernel
    return kernel.astype(BF16), weight.astype(BF16)


def grad_of(sums, feats_t, feat):
    return (-8.0 / feat) * (sums[feat : feat + 1] * feats_t.astype(F32) - sums[:feat])


def backward(grad_t, hid_t, pts, w_out):
    grad_b = grad_t.astype(BF16)
    g_out = dot_nt(hid_t, grad_b)
    hid = hid_t.astype(F32)
    hid_grad = (dot(w_out, grad_b) * (1.0 - hid * hid)).astype(BF16)
    return dot(hid_grad, pts), g_out


def own_kernel(pts, w_in, w_out, va, av, feats, feats1_t, hid_t, av_t, row_sq, prod, grad):
    feat = w_out.shape[1]
    hid_t[...], feats_t, feats1_t[...] = forward(pts[...], w_in[...], w_out[...])
    feats[...] = feats_t.astype(F32).T.astype(BF16)
    av_t[...] = av[...].astype(F32).T.astype(BF16)
    row_sq[...] = half_square(feats[...], 1, feat)
    col_sq = half_square(feats_t, 0, feat)
    n = pts.shape[0]
    for r in range(0, n, CHUNK):
        here = pl.ds(r, CHUNK)
        kernel, weight = kernel_and_weight(
            feats[here, :], row_sq[here, :], av_t[here, :], feats_t, col_sq, va[...], feat
        )
        prod[:, here] = dot_nt(va[...], kernel)
        sums = dot_nt(feats1_t[...], weight)
        grad[:, here] = grad_of(sums, feats_t[:, r : r + CHUNK], feat)


def pair_kernel(
    last, pts_c, va_c, w_in, w_out, feats, feats1_t, av_t, row_sq, va, prod, grad, *refs
):
    if last:
        hid_t, pts, second, g_in_t, g_out, prod_new, prod_c, keep, give, col_prod, col_sums = refs
    else:
        prod_new, prod_c, grad_new, g_in_new, g_out_new, col_prod, col_sums = refs
    feat = w_out.shape[1]
    hid_c, feats_c, feats1_c = forward(pts_c[...], w_in[...], w_out[...])
    col_sq = half_square(feats_c, 0, feat)
    n = pts_c.shape[0]
    grads = []
    for r in range(0, n, CHUNK):
        here = pl.ds(r, CHUNK)
        kernel, weight = kernel_and_weight(
            feats[here, :], row_sq[here, :], av_t[here, :], feats_c, col_sq, va_c[...], feat
        )
        from_rows = dot(va[:, here], kernel)
        sums_rows = dot(feats1_t[:, here], weight)
        if r == 0:
            col_prod[...] = from_rows
            col_sums[...] = sums_rows
        else:
            col_prod[...] += from_rows
            col_sums[...] += sums_rows
        prod_new[:, here] = prod[:, here] + dot_nt(va_c[...], kernel)
        sums = dot_nt(feats1_c, weight)
        total = grad[:, here] + grad_of(sums, feats1_t[:feat, here], feat)
        if last:
            grads.append(total)
        else:
            grad_new[:, here] = total
    prod_c[...] = col_prod[: prod_c.shape[0]]
    gi_c, go_c = backward(grad_of(col_sums[...], feats_c, feat), hid_c, pts_c[...], w_out[...])
    if not last:
        g_in_new[...] = gi_c
        g_out_new[...] = go_c
        return
    gi, go = backward(jnp.concatenate(grads, axis=1), hid_t[...], pts[...], w_out[...])
    g_in = (g_in_t[...] + gi_c + gi).T
    g_o = g_out[...] + go_c + go
    is_second = second[0] == 1
    keep[...] = jnp.where(is_second, g_o, g_in)
    give[...] = jnp.where(is_second, g_in, g_o)


def call(body, ins, outs, scratch=(), smem=None):
    vmem = pl.BlockSpec(memory_space=pltpu.VMEM)
    specs = [pl.BlockSpec(memory_space=pltpu.SMEM) if i == smem else vmem for i in range(len(ins))]
    return pl.pallas_call(
        body,
        out_shape=[jax.ShapeDtypeStruct(s, d) for s, d in outs],
        in_specs=specs,
        out_specs=[vmem] * len(outs),
        scratch_shapes=[pltpu.VMEM(s, d) for s, d in scratch],
        compiler_params=pltpu.CompilerParams(vmem_limit_bytes=32 * 1024 * 1024),
    )(*ins)


def local(points, w_input, w_output, vectors, adjoint):
    nvec, n = vectors.shape
    feat, hid, din = w_output.shape[1], w_output.shape[0], w_input.shape[0]
    blank = jnp.zeros((-2 * nvec % 8, n), BF16)
    va = jnp.concatenate([vectors, adjoint, blank], axis=0)
    av = jnp.concatenate([adjoint, vectors, blank], axis=0)
    k = va.shape[0]
    far_points, far_va = send(points, far_target), send(va, far_target)
    near_points, near_va = send(points, near_target), send(va, near_target)

    feats, feats1_t, hid_t, av_t, row_sq, prod, grad = call(
        own_kernel,
        (points, w_input, w_output, va, av),
        (
            ((n, feat), BF16),
            ((feat + 16, n), BF16),
            ((hid, n), BF16),
            ((n, k), BF16),
            ((n, 1), F32),
            ((k, n), F32),
            ((feat, n), F32),
        ),
    )
    own = (feats, feats1_t, av_t, row_sq, va)
    scratch = (((k, n), F32), ((feat + 16, n), F32))
    prod, near_back, grad, g_in, g_out = call(
        functools.partial(pair_kernel, False),
        (near_points, near_va, w_input, w_output) + own + (prod, grad),
        (((k, n), F32), ((nvec, n), F32), ((feat, n), F32), ((hid, din), F32), ((hid, feat), F32)),
        scratch,
    )
    near_back = send_back(near_back, near_target)
    second = lax.axis_index("c").astype(jnp.int32).reshape(1)
    ins = (far_points, far_va, w_input, w_output) + own + (prod, grad, hid_t, points, second, g_in, g_out)
    prod, far_back, keep, give = call(
        functools.partial(pair_kernel, True),
        ins,
        (((k, n), F32), ((nvec, n), F32), ((hid, feat), F32), ((hid, feat), F32)),
        scratch,
        smem=13,
    )
    mine = keep + swap_cores(give)
    mine = sum_over(mine, ("z",))
    far_back = send_back(far_back, far_target)
    mine = sum_over(mine, ("x", "y"))
    other = swap_cores(mine)
    is_second = second[0] == 1
    grad_input = jnp.where(is_second, other, mine)
    grad_output = jnp.where(is_second, mine, other)
    products = prod[:nvec] + near_back + far_back
    return (products, grad_input, grad_output)


def solution(mesh):
    grid = Mesh(mesh.devices.reshape(4, 4, 8, 2), ALL)
    return jax.shard_map(
        local,
        mesh=grid,
        in_specs=(P(ALL, None), P(), P(), P(None, ALL), P(None, ALL)),
        out_specs=(P(None, ALL), P(), P()),
        check_vma=False,
    )
```

```python
import functools
import math

import jax
import jax.numpy as jnp
from jax import lax
from jax.experimental import pallas as pl
from jax.experimental.pallas import tpu as pltpu
from jax.sharding import Mesh, PartitionSpec as P

ALL = ("x", "y", "z", "c")
CHUNK = 256
LOG2E = math.log2(math.e)
F32 = jnp.float32
BF16 = jnp.bfloat16


def bit(i, k):
    return (i >> k) & 1


def far_target(i):
    return i ^ 8 if bit(i, 3) ^ bit(i, 2) ^ bit(i, 0) == 0 else i ^ 4


def near_target(i):
    return i ^ 1 if bit(i, 1) ^ bit(i, 0) == 0 else i ^ 2


def send(x, target):
    return lax.ppermute(x, ALL, [(i, target(i)) for i in range(lax.axis_size(ALL))])


def send_back(x, target):
    return lax.ppermute(x, ALL, [(target(i), i) for i in range(lax.axis_size(ALL))])


def swap_cores(x):
    return lax.ppermute(x, "c", [(0, 1), (1, 0)])


def sum_over(x, axes):
    n = lax.axis_size(axes)
    sent = jnp.broadcast_to(x.astype(BF16), (n,) + x.shape)
    got = lax.all_to_all(sent, axes, 0, 0)
    return jnp.sum(got.astype(F32), axis=0)


def join(x, masks):
    mine = lax.reduce_precision(x, 8, 7)
    got = [send(mine.astype(BF16), lambda i, m=m: i ^ m).astype(F32) for m in masks]
    if len(masks) == 1:
        return mine + got[0]
    return (mine + got[0]) + (got[1] + got[2])

def dot(a, b):
    return jnp.dot(a, b, preferred_element_type=F32)


def dot_nt(a, b):
    return lax.dot_general(a, b, (((1,), (1,)), ((), ())), preferred_element_type=F32)


def forward(pts, w_in, w_out):
    hid_t = jnp.tanh(dot_nt(w_in.astype(F32).T.astype(BF16), pts)).astype(BF16)
    feats_t = dot(w_out.astype(F32).T.astype(BF16), hid_t).astype(BF16)
    n = pts.shape[0]
    ones = (lax.broadcasted_iota(jnp.int32, (16, n), 0) == 0).astype(F32).astype(BF16)
    return hid_t, feats_t, jnp.concatenate([feats_t, ones], axis=0)


def half_square(feats, axis, feat):
    return jnp.sum(jnp.square(feats.astype(F32)), axis=axis, keepdims=True) * (-LOG2E / (feat / 4.0))


def kernel_and_weight(rows, row_sq, row_av, col_feats_t, col_sq, col_va, feat):
    inner = dot(rows, col_feats_t)
    kernel = jnp.exp2(inner * (2.0 * LOG2E / (feat / 4.0)) + (row_sq + col_sq))
    weight = dot(row_av, col_va) * kernel
    return kernel.astype(BF16), weight.astype(BF16)


def grad_of(sums, feats_t, feat):
    return (-8.0 / feat) * (sums[feat : feat + 1] * feats_t.astype(F32) - sums[:feat])


def backward(grad_t, hid_t, pts, w_out):
    grad_b = grad_t.astype(BF16)
    g_out = dot_nt(hid_t, grad_b)
    hid = hid_t.astype(F32)
    hid_grad = (dot(w_out, grad_b) * (1.0 - hid * hid)).astype(BF16)
    return dot(hid_grad, pts), g_out


def own_kernel(pts, w_in, w_out, va, av, feats, feats1_t, hid_t, av_t, row_sq, prod, grad):
    feat = w_out.shape[1]
    hid_t[...], feats_t, feats1_t[...] = forward(pts[...], w_in[...], w_out[...])
    feats[...] = feats_t.astype(F32).T.astype(BF16)
    av_t[...] = av[...].astype(F32).T.astype(BF16)
    row_sq[...] = half_square(feats[...], 1, feat)
    col_sq = half_square(feats_t, 0, feat)
    n = pts.shape[0]
    for r in range(0, n, CHUNK):
        here = pl.ds(r, CHUNK)
        kernel, weight = kernel_and_weight(
            feats[here, :], row_sq[here, :], av_t[here, :], feats_t, col_sq, va[...], feat
        )
        prod[:, here] = dot_nt(va[...], kernel)
        sums = dot_nt(feats1_t[...], weight)
        grad[:, here] = grad_of(sums, feats_t[:, r : r + CHUNK], feat)


def pair_kernel(
    last, pts_c, va_c, w_in, w_out, feats, feats1_t, av_t, row_sq, va, prod, grad, *refs
):
    if last:
        hid_t, pts, second, g_in_t, g_out, prod_new, prod_c, keep, give, col_prod, col_sums = refs
    else:
        prod_new, prod_c, grad_new, g_in_new, g_out_new, col_prod, col_sums = refs
    feat = w_out.shape[1]
    hid_c, feats_c, feats1_c = forward(pts_c[...], w_in[...], w_out[...])
    col_sq = half_square(feats_c, 0, feat)
    n = pts_c.shape[0]
    grads = []
    for r in range(0, n, CHUNK):
        here = pl.ds(r, CHUNK)
        kernel, weight = kernel_and_weight(
            feats[here, :], row_sq[here, :], av_t[here, :], feats_c, col_sq, va_c[...], feat
        )
        from_rows = dot(va[:, here], kernel)
        sums_rows = dot(feats1_t[:, here], weight)
        if r == 0:
            col_prod[...] = from_rows
            col_sums[...] = sums_rows
        else:
            col_prod[...] += from_rows
            col_sums[...] += sums_rows
        prod_new[:, here] = prod[:, here] + dot_nt(va_c[...], kernel)
        sums = dot_nt(feats1_c, weight)
        total = grad[:, here] + grad_of(sums, feats1_t[:feat, here], feat)
        if last:
            grads.append(total)
        else:
            grad_new[:, here] = total
    prod_c[...] = col_prod[: prod_c.shape[0]]
    gi_c, go_c = backward(grad_of(col_sums[...], feats_c, feat), hid_c, pts_c[...], w_out[...])
    if not last:
        g_in_new[...] = gi_c
        g_out_new[...] = go_c
        return
    gi, go = backward(jnp.concatenate(grads, axis=1), hid_t[...], pts[...], w_out[...])
    g_in = (g_in_t[...] + gi_c + gi).T
    g_o = g_out[...] + go_c + go
    is_second = second[0] == 1
    keep[...] = jnp.where(is_second, g_o, g_in)
    give[...] = jnp.where(is_second, g_in, g_o)


def call(body, ins, outs, scratch=(), smem=None):
    vmem = pl.BlockSpec(memory_space=pltpu.VMEM)
    specs = [pl.BlockSpec(memory_space=pltpu.SMEM) if i == smem else vmem for i in range(len(ins))]
    return pl.pallas_call(
        body,
        out_shape=[jax.ShapeDtypeStruct(s, d) for s, d in outs],
        in_specs=specs,
        out_specs=[vmem] * len(outs),
        scratch_shapes=[pltpu.VMEM(s, d) for s, d in scratch],
        compiler_params=pltpu.CompilerParams(vmem_limit_bytes=16 * 1024 * 1024),
    )(*ins)


def local(points, w_input, w_output, vectors, adjoint):
    nvec, n = vectors.shape
    feat, hid, din = w_output.shape[1], w_output.shape[0], w_input.shape[0]
    blank = jnp.zeros((-2 * nvec % 8, n), BF16)
    va = jnp.concatenate([vectors, adjoint, blank], axis=0)
    av = jnp.concatenate([adjoint, vectors, blank], axis=0)
    k = va.shape[0]
    far_points, far_va = send(points, far_target), send(va, far_target)
    near_points, near_va = send(points, near_target), send(va, near_target)

    feats, feats1_t, hid_t, av_t, row_sq, prod, grad = call(
        own_kernel,
        (points, w_input, w_output, va, av),
        (
            ((n, feat), BF16),
            ((feat + 16, n), BF16),
            ((hid, n), BF16),
            ((n, k), BF16),
            ((n, 1), F32),
            ((k, n), F32),
            ((feat, n), F32),
        ),
    )
    own = (feats, feats1_t, av_t, row_sq, va)
    scratch = (((k, n), F32), ((feat + 16, n), F32))
    prod, near_back, grad, g_in, g_out = call(
        functools.partial(pair_kernel, False),
        (near_points, near_va, w_input, w_output) + own + (prod, grad),
        (((k, n), F32), ((nvec, n), F32), ((feat, n), F32), ((hid, din), F32), ((hid, feat), F32)),
        scratch,
    )
    second = lax.axis_index("c").astype(jnp.int32).reshape(1)
    ins = (far_points, far_va, w_input, w_output) + own + (prod, grad, hid_t, points, second, g_in, g_out)
    prod, far_back, keep, give = call(
        functools.partial(pair_kernel, True),
        ins,
        (((k, n), F32), ((nvec, n), F32), ((hid, feat), F32), ((hid, feat), F32)),
        scratch,
        smem=13,
    )
    mine = keep + swap_cores(give)
    mine = join(mine, [8])
    mine, far_back = lax.optimization_barrier((mine, far_back))
    far_back = send_back(far_back, far_target)
    mine, near_back = lax.optimization_barrier((mine, near_back))
    near_back = send_back(near_back, near_target)
    mine = join(mine, [2, 4, 6])
    mine = sum_over(mine, ('x', 'y'))
    other = swap_cores(mine)
    is_second = second[0] == 1
    grad_input = jnp.where(is_second, other, mine)
    grad_output = jnp.where(is_second, mine, other)
    products = prod[:nvec] + near_back + far_back
    return (products, grad_input, grad_output)


def solution(mesh):
    grid = Mesh(mesh.devices.reshape(4, 4, 8, 2), ALL)
    return jax.shard_map(
        local,
        mesh=grid,
        in_specs=(P(ALL, None), P(), P(), P(None, ALL), P(None, ALL)),
        out_specs=(P(None, ALL), P(), P()),
        check_vma=False,
    )
```

```python
import functools
import math

import jax
import jax.numpy as jnp
from jax import lax
from jax.experimental import pallas as pl
from jax.experimental.pallas import tpu as pltpu
from jax.sharding import Mesh, PartitionSpec as P

ALL = ("x", "y", "z", "c")
CHUNK = 256
LOG2E = math.log2(math.e)
F32 = jnp.float32
BF16 = jnp.bfloat16


def bit(i, k):
    return (i >> k) & 1


def far_target(i):
    return i ^ 8 if bit(i, 3) ^ bit(i, 2) ^ bit(i, 0) == 0 else i ^ 4


def near_target(i):
    return i ^ 1 if bit(i, 1) ^ bit(i, 0) == 0 else i ^ 2


def send(x, target):
    return lax.ppermute(x, ALL, [(i, target(i)) for i in range(lax.axis_size(ALL))])


def send_back(x, target):
    return lax.ppermute(x, ALL, [(target(i), i) for i in range(lax.axis_size(ALL))])


def swap_cores(x):
    return lax.ppermute(x, "c", [(0, 1), (1, 0)])


def sum_over(x, axes):
    n = lax.axis_size(axes)
    sent = jnp.broadcast_to(x.astype(BF16), (n,) + x.shape)
    got = lax.all_to_all(sent, axes, 0, 0)
    return jnp.sum(got.astype(F32), axis=0)


def join(x, masks):
    mine = lax.reduce_precision(x, 8, 7)
    got = [send(mine.astype(BF16), lambda i, m=m: i ^ m).astype(F32) for m in masks]
    if len(masks) == 1:
        return mine + got[0]
    return (mine + got[0]) + (got[1] + got[2])

def dot(a, b):
    return jnp.dot(a, b, preferred_element_type=F32)


def dot_nt(a, b):
    return lax.dot_general(a, b, (((1,), (1,)), ((), ())), preferred_element_type=F32)


def transposed(x):
    return x.astype(F32).T.astype(BF16)


def forward(pts, w_in_t, w_out_t):
    hid_t = jnp.tanh(dot_nt(w_in_t, pts)).astype(BF16)
    feats_t = dot(w_out_t, hid_t).astype(BF16)
    n = pts.shape[0]
    ones = (lax.broadcasted_iota(jnp.int32, (16, n), 0) == 0).astype(F32).astype(BF16)
    return hid_t, feats_t, jnp.concatenate([feats_t, ones], axis=0)


def half_square(feats, axis, feat):
    return jnp.sum(jnp.square(feats.astype(F32)), axis=axis, keepdims=True) * (-LOG2E / (feat / 4.0))


def kernel_rows(rows, row_sq, col_feats_t, col_sq, feat):
    inner = dot(rows, col_feats_t)
    return jnp.exp2(inner * (2.0 * LOG2E / (feat / 4.0)) + (row_sq + col_sq))


def grad_of(sums, feats_t, feat):
    return (-8.0 / feat) * (sums[feat : feat + 1] * feats_t.astype(F32) - sums[:feat])


def backward(grad_t, hid_t, pts, w_out):
    grad_b = grad_t.astype(BF16)
    g_out = dot_nt(hid_t, grad_b)
    hid = hid_t.astype(F32)
    hid_grad = (dot(w_out, grad_b) * (1.0 - hid * hid)).astype(BF16)
    return dot(hid_grad, pts), g_out


def own_kernel(
    pts, w_in, w_out, va, av, w_in_t, w_out_t, feats, feats1_t, hid_t, av_t, row_sq, prod, grad
):
    feat = w_out.shape[1]
    w_in_t[...] = transposed(w_in[...])
    w_out_t[...] = transposed(w_out[...])
    hid_t[...], feats_t, feats1_t[...] = forward(pts[...], w_in_t[...], w_out_t[...])
    feats[...] = transposed(feats_t)
    av_t[...] = transposed(av[...])
    row_sq[...] = half_square(feats[...], 1, feat)
    col_sq = half_square(feats_t, 0, feat)
    n = pts.shape[0]
    for r in range(0, n, CHUNK):
        here = pl.ds(r, CHUNK)
        kernel = kernel_rows(feats[here, :], row_sq[here, :], feats_t, col_sq, feat)
        weight = (dot(av_t[here, :], va[...]) * kernel).astype(BF16)
        prod[:, here] = dot_nt(va[...], kernel.astype(BF16))
        sums = dot_nt(feats1_t[...], weight)
        grad[:, here] = grad_of(sums, feats_t[:, r : r + CHUNK], feat)


def meet_kernel(pts_c, w_in_t, w_out_t, feats, row_sq, va, hid_c, feats1_c, kernel, prod_c):
    n, feat = feats.shape
    hid_c[...], feats_c, feats1_c[...] = forward(pts_c[...], w_in_t[...], w_out_t[...])
    col_sq = half_square(feats_c, 0, feat)
    for r in range(0, n, CHUNK):
        here = pl.ds(r, CHUNK)
        kernel[here, :] = kernel_rows(
            feats[here, :], row_sq[here, :], feats_c, col_sq, feat
        ).astype(BF16)
    for r in range(0, n, CHUNK):
        here = pl.ds(r, CHUNK)
        prod_c[:, here] = dot(va[...], kernel[:, here])[: prod_c.shape[0]]


def pair_kernel(
    last, pts_c, va_c, hid_c, feats1_c, kernel, w_out, feats1_t, av_t, prod, grad, *refs
):
    if last:
        hid_t, pts, second, g_in_t, g_out, prod_new, keep, give, weight = refs
    else:
        prod_new, grad_new, g_in_new, g_out_new, weight = refs
    feat = w_out.shape[1]
    n = pts_c.shape[0]
    grads = []
    for r in range(0, n, CHUNK):
        here = pl.ds(r, CHUNK)
        pairing = dot(av_t[here, :], va_c[...])
        weight[here, :] = (pairing * kernel[here, :].astype(F32)).astype(BF16)
        prod_new[:, here] = prod[:, here] + dot_nt(va_c[...], kernel[here, :])
        sums = dot_nt(feats1_c[...], weight[here, :])
        total = grad[:, here] + grad_of(sums, feats1_t[:feat, here], feat)
        if last:
            grads.append(total)
        else:
            grad_new[:, here] = total
    grads_c = []
    for r in range(0, n, CHUNK):
        here = pl.ds(r, CHUNK)
        grads_c.append(grad_of(dot(feats1_t[...], weight[:, here]), feats1_c[:feat, here], feat))
    gi_c, go_c = backward(jnp.concatenate(grads_c, axis=1), hid_c[...], pts_c[...], w_out[...])
    if not last:
        g_in_new[...] = gi_c
        g_out_new[...] = go_c
        return
    gi, go = backward(jnp.concatenate(grads, axis=1), hid_t[...], pts[...], w_out[...])
    g_in = (g_in_t[...] + gi_c + gi).T
    g_o = g_out[...] + go_c + go
    is_second = second[0] == 1
    keep[...] = jnp.where(is_second, g_o, g_in)
    give[...] = jnp.where(is_second, g_in, g_o)


def call(body, ins, outs, scratch=(), smem=None):
    vmem = pl.BlockSpec(memory_space=pltpu.VMEM)
    specs = [pl.BlockSpec(memory_space=pltpu.SMEM) if i == smem else vmem for i in range(len(ins))]
    return pl.pallas_call(
        body,
        out_shape=[jax.ShapeDtypeStruct(s, d) for s, d in outs],
        in_specs=specs,
        out_specs=[vmem] * len(outs),
        scratch_shapes=[pltpu.VMEM(s, d) for s, d in scratch],
        compiler_params=pltpu.CompilerParams(vmem_limit_bytes=16 * 1024 * 1024),
    )(*ins)


def local(points, w_input, w_output, vectors, adjoint):
    nvec, n = vectors.shape
    feat, hid, din = w_output.shape[1], w_output.shape[0], w_input.shape[0]
    blank = jnp.zeros((-2 * nvec % 8, n), BF16)
    va = jnp.concatenate([vectors, adjoint, blank], axis=0)
    av = jnp.concatenate([adjoint, vectors, blank], axis=0)
    k = va.shape[0]
    far_points, far_va = send(points, far_target), send(va, far_target)
    near_points, near_va = send(points, near_target), send(va, near_target)

    w_in_t, w_out_t, feats, feats1_t, hid_t, av_t, row_sq, prod, grad = call(
        own_kernel,
        (points, w_input, w_output, va, av),
        (
            ((hid, din), BF16),
            ((feat, hid), BF16),
            ((n, feat), BF16),
            ((feat + 16, n), BF16),
            ((hid, n), BF16),
            ((n, k), BF16),
            ((n, 1), F32),
            ((k, n), F32),
            ((feat, n), F32),
        ),
    )

    def meet(block_points):
        return call(
            meet_kernel,
            (block_points, w_in_t, w_out_t, feats, row_sq, va),
            (((hid, n), BF16), ((feat + 16, n), BF16), ((n, n), BF16), ((nvec, n), F32)),
        )

    scratch = (((n, n), BF16),)
    hid_c, feats1_c, kernel, near_back = meet(near_points)
    prod, grad, g_in, g_out = call(
        functools.partial(pair_kernel, False),
        (near_points, near_va, hid_c, feats1_c, kernel, w_output, feats1_t, av_t, prod, grad),
        (((k, n), F32), ((feat, n), F32), ((hid, din), F32), ((hid, feat), F32)),
        scratch,
    )
    second = lax.axis_index("c").astype(jnp.int32).reshape(1)
    prod, late_points = lax.optimization_barrier((prod, far_points))
    hid_c, feats1_c, kernel, far_back = meet(late_points)
    prod, keep, give = call(
        functools.partial(pair_kernel, True),
        (late_points, far_va, hid_c, feats1_c, kernel, w_output, feats1_t, av_t, prod, grad)
        + (hid_t, points, second, g_in, g_out),
        (((k, n), F32), ((hid, feat), F32), ((hid, feat), F32)),
        scratch,
        smem=12,
    )
    mine = keep + swap_cores(give)
    mine = join(mine, [8])
    mine, far_back = lax.optimization_barrier((mine, far_back))
    far_back = send_back(far_back, far_target)
    mine, near_back = lax.optimization_barrier((mine, near_back))
    near_back = send_back(near_back, near_target)
    mine = join(mine, [2, 4, 6])
    mine = sum_over(mine, ('x', 'y'))
    other = swap_cores(mine)
    is_second = second[0] == 1
    grad_input = jnp.where(is_second, other, mine)
    grad_output = jnp.where(is_second, mine, other)
    products = prod[:nvec] + near_back + far_back
    return (products, grad_input, grad_output)


def solution(mesh):
    grid = Mesh(mesh.devices.reshape(4, 4, 8, 2), ALL)
    return jax.shard_map(
        local,
        mesh=grid,
        in_specs=(P(ALL, None), P(), P(), P(None, ALL), P(None, ALL)),
        out_specs=(P(None, ALL), P(), P()),
        check_vma=False,
    )
```

```python
import functools
import math

import jax
import jax.numpy as jnp
from jax import lax
from jax.experimental import pallas as pl
from jax.experimental.pallas import tpu as pltpu
from jax.sharding import Mesh, PartitionSpec as P

ALL = ("x", "y", "z", "c")
CHUNK = 256
LOG2E = math.log2(math.e)
F32 = jnp.float32
BF16 = jnp.bfloat16


def bit(i, k):
    return (i >> k) & 1


def far_target(i):
    return i ^ 8 if bit(i, 3) ^ bit(i, 2) ^ bit(i, 0) == 1 else i ^ 4


def near_target(i):
    return i ^ 1 if bit(i, 1) ^ bit(i, 0) == 0 else i ^ 2


def send(x, target):
    return lax.ppermute(x, ALL, [(i, target(i)) for i in range(lax.axis_size(ALL))])


def send_back(x, target):
    return lax.ppermute(x, ALL, [(target(i), i) for i in range(lax.axis_size(ALL))])


def swap_cores(x):
    return lax.ppermute(x, "c", [(0, 1), (1, 0)])


def sum_over(x, axes):
    n = lax.axis_size(axes)
    sent = jnp.broadcast_to(x.astype(BF16), (n,) + x.shape)
    got = lax.all_to_all(sent, axes, 0, 0)
    return jnp.sum(got.astype(F32), axis=0)


def join(x, masks):
    mine = lax.reduce_precision(x, 8, 7)
    got = [send(mine.astype(BF16), lambda i, m=m: i ^ m).astype(F32) for m in masks]
    if len(masks) == 1:
        return mine + got[0]
    return (mine + got[0]) + (got[1] + got[2])

def dot(a, b):
    return jnp.dot(a, b, preferred_element_type=F32)


def dot_nt(a, b):
    return lax.dot_general(a, b, (((1,), (1,)), ((), ())), preferred_element_type=F32)


def transposed(x):
    return x.astype(F32).T.astype(BF16)


def forward(pts, w_in_t, w_out_t):
    hid_t = jnp.tanh(dot_nt(w_in_t, pts)).astype(BF16)
    feats_t = dot(w_out_t, hid_t).astype(BF16)
    n = pts.shape[0]
    ones = (lax.broadcasted_iota(jnp.int32, (16, n), 0) == 0).astype(F32).astype(BF16)
    return hid_t, feats_t, jnp.concatenate([feats_t, ones], axis=0)


def half_square(feats, axis, feat):
    return jnp.sum(jnp.square(feats.astype(F32)), axis=axis, keepdims=True) * (-LOG2E / (feat / 4.0))


def kernel_rows(rows, row_sq, col_feats_t, col_sq, feat):
    inner = dot(rows, col_feats_t)
    return jnp.exp2(inner * (2.0 * LOG2E / (feat / 4.0)) + (row_sq + col_sq))


def grad_of(sums, feats_t, feat):
    return (-8.0 / feat) * (sums[feat : feat + 1] * feats_t.astype(F32) - sums[:feat])


def backward(grad_t, hid_t, pts, w_out):
    grad_b = grad_t.astype(BF16)
    g_out = dot_nt(hid_t, grad_b)
    hid = hid_t.astype(F32)
    hid_grad = (dot(w_out, grad_b) * (1.0 - hid * hid)).astype(BF16)
    return dot(hid_grad, pts), g_out


def own_kernel(
    pts, w_in, w_out, va, av, w_in_t, w_out_t, feats, feats1_t, hid_t, av_t, row_sq, prod, grad
):
    feat = w_out.shape[1]
    w_in_t[...] = transposed(w_in[...])
    w_out_t[...] = transposed(w_out[...])
    hid_t[...], feats_t, feats1_t[...] = forward(pts[...], w_in_t[...], w_out_t[...])
    feats[...] = transposed(feats_t)
    av_t[...] = transposed(av[...])
    row_sq[...] = half_square(feats[...], 1, feat)
    col_sq = half_square(feats_t, 0, feat)
    n = pts.shape[0]
    for r in range(0, n, CHUNK):
        here = pl.ds(r, CHUNK)
        kernel = kernel_rows(feats[here, :], row_sq[here, :], feats_t, col_sq, feat)
        weight = (dot(av_t[here, :], va[...]) * kernel).astype(BF16)
        prod[:, here] = dot_nt(va[...], kernel.astype(BF16))
        sums = dot_nt(feats1_t[...], weight)
        grad[:, here] = grad_of(sums, feats_t[:, r : r + CHUNK], feat)


def meet_kernel(pts_c, w_in_t, w_out_t, feats, row_sq, va, hid_c, feats1_c, kernel, prod_c):
    n, feat = feats.shape
    hid_c[...], feats_c, feats1_c[...] = forward(pts_c[...], w_in_t[...], w_out_t[...])
    col_sq = half_square(feats_c, 0, feat)
    for r in range(0, n, CHUNK):
        here = pl.ds(r, CHUNK)
        kernel[here, :] = kernel_rows(
            feats[here, :], row_sq[here, :], feats_c, col_sq, feat
        ).astype(BF16)
    for r in range(0, n, CHUNK):
        here = pl.ds(r, CHUNK)
        prod_c[:, here] = dot(va[...], kernel[:, here])[: prod_c.shape[0]]


def pair_kernel(
    last, pts_c, va_c, hid_c, feats1_c, kernel, w_out, feats1_t, av_t, prod, grad, *refs
):
    if last:
        hid_t, pts, second, g_in_t, g_out, prod_new, keep, give, weight = refs
    else:
        prod_new, grad_new, g_in_new, g_out_new, weight = refs
    feat = w_out.shape[1]
    n = pts_c.shape[0]
    grads = []
    for r in range(0, n, CHUNK):
        here = pl.ds(r, CHUNK)
        pairing = dot(av_t[here, :], va_c[...])
        weight[here, :] = (pairing * kernel[here, :].astype(F32)).astype(BF16)
        prod_new[:, here] = prod[:, here] + dot_nt(va_c[...], kernel[here, :])
        sums = dot_nt(feats1_c[...], weight[here, :])
        total = grad[:, here] + grad_of(sums, feats1_t[:feat, here], feat)
        if last:
            grads.append(total)
        else:
            grad_new[:, here] = total
    grads_c = []
    for r in range(0, n, CHUNK):
        here = pl.ds(r, CHUNK)
        grads_c.append(grad_of(dot(feats1_t[...], weight[:, here]), feats1_c[:feat, here], feat))
    gi_c, go_c = backward(jnp.concatenate(grads_c, axis=1), hid_c[...], pts_c[...], w_out[...])
    if not last:
        g_in_new[...] = gi_c
        g_out_new[...] = go_c
        return
    gi, go = backward(jnp.concatenate(grads, axis=1), hid_t[...], pts[...], w_out[...])
    g_in = (g_in_t[...] + gi_c + gi).T
    g_o = g_out[...] + go_c + go
    is_second = second[0] == 1
    keep[...] = jnp.where(is_second, g_o, g_in)
    give[...] = jnp.where(is_second, g_in, g_o)


def call(body, ins, outs, scratch=(), smem=None):
    vmem = pl.BlockSpec(memory_space=pltpu.VMEM)
    specs = [pl.BlockSpec(memory_space=pltpu.SMEM) if i == smem else vmem for i in range(len(ins))]
    return pl.pallas_call(
        body,
        out_shape=[jax.ShapeDtypeStruct(s, d) for s, d in outs],
        in_specs=specs,
        out_specs=[vmem] * len(outs),
        scratch_shapes=[pltpu.VMEM(s, d) for s, d in scratch],
        compiler_params=pltpu.CompilerParams(vmem_limit_bytes=16 * 1024 * 1024),
    )(*ins)


def local(points, w_input, w_output, vectors, adjoint):
    nvec, n = vectors.shape
    feat, hid, din = w_output.shape[1], w_output.shape[0], w_input.shape[0]
    blank = jnp.zeros((-2 * nvec % 8, n), BF16)
    va = jnp.concatenate([vectors, adjoint, blank], axis=0)
    av = jnp.concatenate([adjoint, vectors, blank], axis=0)
    k = va.shape[0]
    far_points, far_va = send(points, far_target), send(va, far_target)
    near_points, near_va = send(points, near_target), send(va, near_target)

    w_in_t, w_out_t, feats, feats1_t, hid_t, av_t, row_sq, prod, grad = call(
        own_kernel,
        (points, w_input, w_output, va, av),
        (
            ((hid, din), BF16),
            ((feat, hid), BF16),
            ((n, feat), BF16),
            ((feat + 16, n), BF16),
            ((hid, n), BF16),
            ((n, k), BF16),
            ((n, 1), F32),
            ((k, n), F32),
            ((feat, n), F32),
        ),
    )

    def meet(block_points):
        return call(
            meet_kernel,
            (block_points, w_in_t, w_out_t, feats, row_sq, va),
            (((hid, n), BF16), ((feat + 16, n), BF16), ((n, n), BF16), ((nvec, n), F32)),
        )

    scratch = (((n, n), BF16),)
    hid_c, feats1_c, kernel, near_back = meet(near_points)
    prod, grad, g_in, g_out = call(
        functools.partial(pair_kernel, False),
        (near_points, near_va, hid_c, feats1_c, kernel, w_output, feats1_t, av_t, prod, grad),
        (((k, n), F32), ((feat, n), F32), ((hid, din), F32), ((hid, feat), F32)),
        scratch,
    )
    second = lax.axis_index("c").astype(jnp.int32).reshape(1)
    near_back = send_back(near_back, near_target)
    prod, late_points = lax.optimization_barrier((prod, far_points))
    hid_c, feats1_c, kernel, far_back = meet(late_points)
    prod, keep, give = call(
        functools.partial(pair_kernel, True),
        (late_points, far_va, hid_c, feats1_c, kernel, w_output, feats1_t, av_t, prod, grad)
        + (hid_t, points, second, g_in, g_out),
        (((k, n), F32), ((hid, feat), F32), ((hid, feat), F32)),
        scratch,
        smem=12,
    )
    mine = keep + swap_cores(give)
    far_back = send_back(far_back, far_target)
    mine = join(mine, [8])
    mine = join(mine, [2, 4, 6])
    mine = sum_over(mine, ('x', 'y'))
    other = swap_cores(mine)
    is_second = second[0] == 1
    grad_input = jnp.where(is_second, other, mine)
    grad_output = jnp.where(is_second, mine, other)
    products = prod[:nvec] + near_back + far_back
    return (products, grad_input, grad_output)


def solution(mesh):
    grid = Mesh(mesh.devices.reshape(4, 4, 8, 2), ALL)
    return jax.shard_map(
        local,
        mesh=grid,
        in_specs=(P(ALL, None), P(), P(), P(None, ALL), P(None, ALL)),
        out_specs=(P(None, ALL), P(), P()),
        check_vma=False,
    )
```

```python
import functools
import math

import jax
import jax.numpy as jnp
from jax import lax
from jax.experimental import pallas as pl
from jax.experimental.pallas import tpu as pltpu
from jax.sharding import Mesh, PartitionSpec as P

ALL = ("x", "y", "z", "c")
CHUNK = 256
LOG2E = math.log2(math.e)
F32 = jnp.float32
BF16 = jnp.bfloat16


def bit(i, k):
    return (i >> k) & 1


def far_target(i):
    return i ^ 8 if bit(i, 3) ^ bit(i, 2) ^ bit(i, 0) == 1 else i ^ 4


def near_target(i):
    return i ^ 1 if bit(i, 1) ^ bit(i, 0) == 0 else i ^ 2


def send(x, target):
    return lax.ppermute(x, ALL, [(i, target(i)) for i in range(lax.axis_size(ALL))])


def send_back(x, target):
    return lax.ppermute(x, ALL, [(target(i), i) for i in range(lax.axis_size(ALL))])


def swap_cores(x):
    return lax.ppermute(x, "c", [(0, 1), (1, 0)])


def sum_over(x, axes):
    n = lax.axis_size(axes)
    sent = jnp.broadcast_to(x.astype(BF16), (n,) + x.shape)
    got = lax.all_to_all(sent, axes, 0, 0)
    return jnp.sum(got.astype(F32), axis=0)


def join(x, masks):
    mine = lax.reduce_precision(x, 8, 7)
    got = [send(mine.astype(BF16), lambda i, m=m: i ^ m).astype(F32) for m in masks]
    if len(masks) == 1:
        return mine + got[0]
    return (mine + got[0]) + (got[1] + got[2])

def dot(a, b):
    return jnp.dot(a, b, preferred_element_type=F32)


def dot_nt(a, b):
    return lax.dot_general(a, b, (((1,), (1,)), ((), ())), preferred_element_type=F32)


def tiles_up(rows):
    return -(-rows // 16) * 16


def transposed(x):
    return x.astype(F32).T.astype(BF16)


def forward(pts, w_in_t, w_out_t):
    hid_t = jnp.tanh(dot_nt(w_in_t, pts)).astype(BF16)
    feats_t = dot(w_out_t, hid_t).astype(BF16)
    n = pts.shape[0]
    ones = (lax.broadcasted_iota(jnp.int32, (16, n), 0) == 0).astype(F32).astype(BF16)
    return hid_t, feats_t, jnp.concatenate([feats_t, ones], axis=0)


def half_square(feats, axis, feat):
    return jnp.sum(jnp.square(feats.astype(F32)), axis=axis, keepdims=True) * (-LOG2E / (feat / 4.0))


def kernel_rows(rows, row_sq, col_feats_t, col_sq, feat):
    inner = dot(rows, col_feats_t)
    return jnp.exp2(inner * (2.0 * LOG2E / (feat / 4.0)) + (row_sq + col_sq))


def grad_of(sums, feats_t, feat):
    return (-8.0 / feat) * (sums[feat : feat + 1] * feats_t.astype(F32) - sums[:feat])


def backward(grad_t, hid_t, pts, w_out):
    grad_b = grad_t.astype(BF16)
    g_out = dot_nt(hid_t, grad_b)
    hid = hid_t.astype(F32)
    hid_grad = (dot(w_out, grad_b) * (1.0 - hid * hid)).astype(BF16)
    return dot(hid_grad, pts), g_out


def own_kernel(
    pts, w_in, w_out, va, av, w_in_t, w_out_t, feats, feats1_t, hid_t, av_t, row_sq, prod, grad
):
    feat = w_out.shape[1]
    w_in_t[...] = transposed(w_in[...])
    w_out_t[...] = transposed(w_out[...])
    hid_t[...], feats_t, feats1_t[...] = forward(pts[...], w_in_t[...], w_out_t[...])
    feats[...] = transposed(feats_t)
    av_t[...] = transposed(av[...])
    row_sq[...] = half_square(feats[...], 1, feat)
    col_sq = half_square(feats_t, 0, feat)
    n = pts.shape[0]
    for r in range(0, n, CHUNK):
        here = pl.ds(r, CHUNK)
        kernel = kernel_rows(feats[here, :], row_sq[here, :], feats_t, col_sq, feat)
        weight = (dot(av_t[here, :], va[...]) * kernel).astype(BF16)
        prod[:, here] = dot_nt(va[: prod.shape[0], :], kernel.astype(BF16))
        sums = dot_nt(feats1_t[...], weight)
        grad[:, here] = grad_of(sums, feats_t[:, r : r + CHUNK], feat)


def meet_kernel(pts_c, w_in_t, w_out_t, feats, row_sq, va, hid_c, feats1_c, kernel, prod_c):
    n, feat = feats.shape
    hid_c[...], feats_c, feats1_c[...] = forward(pts_c[...], w_in_t[...], w_out_t[...])
    col_sq = half_square(feats_c, 0, feat)
    for r in range(0, n, CHUNK):
        here = pl.ds(r, CHUNK)
        kernel[here, :] = kernel_rows(
            feats[here, :], row_sq[here, :], feats_c, col_sq, feat
        ).astype(BF16)
    for r in range(0, n, CHUNK):
        here = pl.ds(r, CHUNK)
        prod_c[:, here] = dot(va[: tiles_up(prod_c.shape[0]), :], kernel[:, here])[: prod_c.shape[0]]


def pair_kernel(
    last, pts_c, va_c, hid_c, feats1_c, kernel, w_out, feats1_t, av_t, prod, grad, *refs
):
    if last:
        hid_t, pts, second, g_in_t, g_out, prod_new, keep, give, weight = refs
    else:
        prod_new, grad_new, g_in_new, g_out_new, weight = refs
    feat = w_out.shape[1]
    n = pts_c.shape[0]
    grads = []
    for r in range(0, n, CHUNK):
        here = pl.ds(r, CHUNK)
        pairing = dot(av_t[here, :], va_c[...])
        weight[here, :] = (pairing * kernel[here, :].astype(F32)).astype(BF16)
        prod_new[:, here] = prod[:, here] + dot_nt(va_c[: prod.shape[0], :], kernel[here, :])
        sums = dot_nt(feats1_c[...], weight[here, :])
        total = grad[:, here] + grad_of(sums, feats1_t[:feat, here], feat)
        if last:
            grads.append(total)
        else:
            grad_new[:, here] = total
    grads_c = []
    for r in range(0, n, CHUNK):
        here = pl.ds(r, CHUNK)
        grads_c.append(grad_of(dot(feats1_t[...], weight[:, here]), feats1_c[:feat, here], feat))
    gi_c, go_c = backward(jnp.concatenate(grads_c, axis=1), hid_c[...], pts_c[...], w_out[...])
    if not last:
        g_in_new[...] = gi_c
        g_out_new[...] = go_c
        return
    gi, go = backward(jnp.concatenate(grads, axis=1), hid_t[...], pts[...], w_out[...])
    g_in = (g_in_t[...] + gi_c + gi).T
    g_o = g_out[...] + go_c + go
    is_second = second[0] == 1
    keep[...] = jnp.where(is_second, g_o, g_in)
    give[...] = jnp.where(is_second, g_in, g_o)


def call(body, ins, outs, scratch=(), smem=None):
    vmem = pl.BlockSpec(memory_space=pltpu.VMEM)
    specs = [pl.BlockSpec(memory_space=pltpu.SMEM) if i == smem else vmem for i in range(len(ins))]
    return pl.pallas_call(
        body,
        out_shape=[jax.ShapeDtypeStruct(s, d) for s, d in outs],
        in_specs=specs,
        out_specs=[vmem] * len(outs),
        scratch_shapes=[pltpu.VMEM(s, d) for s, d in scratch],
        compiler_params=pltpu.CompilerParams(vmem_limit_bytes=16 * 1024 * 1024),
    )(*ins)


def local(points, w_input, w_output, vectors, adjoint):
    nvec, n = vectors.shape
    feat, hid, din = w_output.shape[1], w_output.shape[0], w_input.shape[0]
    blank = jnp.zeros((-2 * nvec % 8, n), BF16)
    va = jnp.concatenate([vectors, adjoint, blank], axis=0)
    av = jnp.concatenate([adjoint, vectors, blank], axis=0)
    k = va.shape[0]
    near_points = send(points, near_target)
    va, later_points = lax.optimization_barrier((va, points))
    near_va = send(va, near_target)
    far_points, far_va = send(later_points, far_target), send(va, far_target)

    w_in_t, w_out_t, feats, feats1_t, hid_t, av_t, row_sq, prod, grad = call(
        own_kernel,
        (points, w_input, w_output, va, av),
        (
            ((hid, din), BF16),
            ((feat, hid), BF16),
            ((n, feat), BF16),
            ((feat + 16, n), BF16),
            ((hid, n), BF16),
            ((n, k), BF16),
            ((n, 1), F32),
            ((tiles_up(nvec), n), F32),
            ((feat, n), F32),
        ),
    )

    def meet(block_points):
        return call(
            meet_kernel,
            (block_points, w_in_t, w_out_t, feats, row_sq, va),
            (((hid, n), BF16), ((feat + 16, n), BF16), ((n, n), BF16), ((nvec, n), F32)),
        )

    scratch = (((n, n), BF16),)
    hid_c, feats1_c, kernel, near_back = meet(near_points)
    prod, grad, g_in, g_out = call(
        functools.partial(pair_kernel, False),
        (near_points, near_va, hid_c, feats1_c, kernel, w_output, feats1_t, av_t, prod, grad),
        (((tiles_up(nvec), n), F32), ((feat, n), F32), ((hid, din), F32), ((hid, feat), F32)),
        scratch,
    )
    second = lax.axis_index("c").astype(jnp.int32).reshape(1)
    near_back = send_back(near_back, near_target)
    prod, late_points = lax.optimization_barrier((prod, far_points))
    hid_c, feats1_c, kernel, far_back = meet(late_points)
    prod, keep, give = call(
        functools.partial(pair_kernel, True),
        (late_points, far_va, hid_c, feats1_c, kernel, w_output, feats1_t, av_t, prod, grad)
        + (hid_t, points, second, g_in, g_out),
        (((tiles_up(nvec), n), F32), ((hid, feat), F32), ((hid, feat), F32)),
        scratch,
        smem=12,
    )
    mine = keep + swap_cores(give)
    far_back = send_back(far_back, far_target)
    mine = join(mine, [8])
    mine = join(mine, [2, 4, 6])
    mine = sum_over(mine, ('x', 'y'))
    other = swap_cores(mine)
    is_second = second[0] == 1
    grad_input = jnp.where(is_second, other, mine)
    grad_output = jnp.where(is_second, mine, other)
    products = prod[:nvec] + near_back + far_back
    return (products, grad_input, grad_output)


def solution(mesh):
    grid = Mesh(mesh.devices.reshape(4, 4, 8, 2), ALL)
    return jax.shard_map(
        local,
        mesh=grid,
        in_specs=(P(ALL, None), P(), P(), P(None, ALL), P(None, ALL)),
        out_specs=(P(None, ALL), P(), P()),
        check_vma=False,
    )
```
